32 devices in a mesh: dp: 16 (over z, x, core), tensor: 2 (over y).
Axes of the slice: x: 2, y: 2, z: 4, core: 2. Of those that a mesh axis runs over, the one named last changes fastest.
Arguments:
- tokens: bfloat16 [32768, 1024], P(('dp', 'tensor')), may hold values from -6 to 6
- cotangent: bfloat16 [32768, 1024], P(('dp', 'tensor')), may hold values from -6 to 6
- seq_lengths: int32 [16, 8], P('dp'), may hold values from 0 to 2048, as said below
- qkv_weight: float32 [3, 1024, 1024], P(None, None, 'tensor'), may hold values from -0.1875 to 0.1875
- qkv_mean: float32 [3, 1024, 1024], P(None, None, 'tensor'), may hold values from -712.3979 to 712.3979
- qkv_square: float32 [3, 1024, 1024], P(None, None, 'tensor'), may hold values from 294.912 to 419430.4
- proj_weight: float32 [1024, 1024], P('tensor'), may hold values from -2 to 2
- proj_mean: float32 [1024, 1024], P('tensor'), may hold values from -4 to 4
- proj_square: float32 [1024, 1024], P('tensor'), may hold values from 1.92 to 30.72
- inner_weight: float32 [2, 1024, 2624], P(None, None, 'tensor'), may hold values from -0.1875 to 0.1875
- inner_mean: float32 [2, 1024, 2624], P(None, None, 'tensor'), may hold values from -40 to 40
- inner_square: float32 [2, 1024, 2624], P(None, None, 'tensor'), may hold values from 32.768 to 524.288
- down_weight: float32 [2624, 1024], P('tensor'), may hold values from -0.125 to 0.125
- down_mean: float32 [2624, 1024], P('tensor'), may hold values from -64 to 64
- down_square: float32 [2624, 1024], P('tensor'), may hold values from 81.92 to 1310.72
- norm_gains: float32 [2, 1024], replicated, may hold values from 0.5 to 1.5
- gains_mean: float32 [2, 1024], replicated, may hold values from -112.64 to 112.64
- gains_square: float32 [2, 1024], replicated, may hold values from 163.84 to 10485.76
Outputs:
- layer_out: bfloat16 [32768, 1024], P(('dp', 'tensor'))
- input_grad: float32 [32768, 1024], P(('dp', 'tensor'))
- qkv_first: float32 [3, 1024, 1024], P(None, None, 'tensor')
- qkv_second: float32 [3, 1024, 1024], P(None, None, 'tensor')
- qkv_updated: float32 [3, 1024, 1024], P(None, None, 'tensor')
- proj_first: float32 [1024, 1024], P('tensor')
- proj_second: float32 [1024, 1024], P('tensor')
- proj_updated: float32 [1024, 1024], P('tensor')
- inner_first: float32 [2, 1024, 2624], P(None, None, 'tensor')
- inner_second: float32 [2, 1024, 2624], P(None, None, 'tensor')
- inner_updated: float32 [2, 1024, 2624], P(None, None, 'tensor')
- down_first: float32 [2624, 1024], P('tensor')
- down_second: float32 [2624, 1024], P('tensor')
- down_updated: float32 [2624, 1024], P('tensor')
- gains_first: float32 [2, 1024], replicated
- gains_second: float32 [2, 1024], replicated
- gains_updated: float32 [2, 1024], replicated
The draws below stay inside these ranges and needn't reach their ends.
Inputs may be any that keep to these rules, and one draw needn't show every extreme that they name: `seq_lengths`: A dp index's lengths sum to at most 2048; empty slots have length 0; in every draw one dp index holds a single sequence of exactly 2048 tokens.
All inputs are finite; a program needn't handle non-finite values.
Results may differ from the reference program's by a relative error of at most 0.024.
Values may be sent and summed in bfloat16 or wider, within the bound.
A program may use at most 384 MiB of HBM per device.

```python
import math
import jax
import jax.numpy as jnp
from jax import lax

D = 1024
HEADS = 16
HEAD_DIM = 64
FF = 2624
CAP = 2048
SEQS = 8
STEP = 10
TOKENS = 32768
N_DP = 16


def draw_seq_lengths(key, part):
    key = jax.random.fold_in(key, 1)
    key_total, key_count, key_weight, key_full = jax.random.split(key, 4)
    devices = TOKENS // CAP
    totals = jax.random.randint(key_total, (devices,), CAP // 8, CAP + 1)
    counts = jax.random.randint(key_count, (devices,), 1, SEQS + 1)
    weights = jax.random.randint(key_weight, (devices, SEQS), 1, 17)
    slot_ids = jnp.arange(SEQS)
    weights = jnp.where(slot_ids[None, :] < counts[:, None], weights, 0)
    lengths = totals[:, None] * weights // jnp.sum(weights, axis=1, keepdims=True)
    chosen = jax.random.randint(key_full, (), 0, devices)
    full_row = jnp.where(slot_ids == 0, CAP, 0)
    lengths = jnp.where(jnp.arange(devices)[:, None] == chosen, full_row[None, :], lengths)
    return lengths.astype(jnp.int32)


def moment_draw(key, shape, factors):
    level = jnp.array(factors, dtype=jnp.float32) * TOKENS
    scale = 0.11 * jnp.sqrt(level)
    noise = jax.random.truncated_normal(key, -4.0, 4.0, shape, jnp.float32)
    return noise * scale.reshape((shape[0],) + (1,) * (len(shape) - 1))


def square_draw(key, shape, factors):
    level = jnp.array(factors, dtype=jnp.float32) * TOKENS
    spread = jnp.exp(jax.random.uniform(key, shape, jnp.float32, math.log(0.01), math.log(0.16)))
    return spread * level.reshape((shape[0],) + (1,) * (len(shape) - 1))


def draw_qkv_mean(key, part):
    key = jax.random.fold_in(key, 2)
    return moment_draw(key, (3, D, D), [80.0, 80.0, 0.9])


def draw_qkv_square(key, part):
    key = jax.random.fold_in(key, 3)
    return square_draw(key, (3, D, D), [80.0, 80.0, 0.9])


def draw_gains_mean(key, part):
    key = jax.random.fold_in(key, 4)
    return moment_draw(key, (2, D), [2.0, 0.5])


def draw_gains_square(key, part):
    key = jax.random.fold_in(key, 5)
    return square_draw(key, (2, D), [2.0, 0.5])


def block_scale(own_key, shape, shards, least, high):
    def one(axis_at, blocks):
        steps = jax.random.uniform(jax.random.fold_in(jax.random.fold_in(own_key, 6), axis_at), (blocks,), jnp.float32, least / len(shards), high / len(shards))
        return jnp.repeat(jnp.exp(steps), shape[axis_at] // blocks).reshape((-1,) + (1,) * (len(shape) - axis_at - 1))

    factor_of = one(*shards[0])
    for cut in shards[1:]:
        factor_of = factor_of * one(*cut)
    return factor_of


def bell_draw(stream_key, extent, deviation, bound, cuts=(), kind=jnp.bfloat16):
    entries = deviation * jax.random.normal(stream_key, extent, jnp.float32)
    if cuts:
        entries = entries * block_scale(stream_key, extent, cuts, -0.22, 0.18)
    return jnp.clip(entries, -bound, bound).astype(kind)


def setup_inputs(seed: int = 0) -> dict:
    splits = jax.random.split(jax.random.key(seed), 19)
    return {
        "tokens": bell_draw(splits[0], (TOKENS, D), 1.0, 6.0, ((0, 32),)),
        "cotangent": bell_draw(splits[1], (TOKENS, D), 1.0, 6.0, ((0, 32),)),
        "seq_lengths": draw_seq_lengths(jax.random.fold_in(splits[18], 71), 0),
        "qkv_weight": bell_draw(splits[3], (3, D, D), D ** -0.5, 0.1875, ((2, 2),), jnp.float32),
        "qkv_mean": draw_qkv_mean(jax.random.fold_in(splits[18], 71), 0),
        "qkv_square": draw_qkv_square(jax.random.fold_in(splits[18], 71), 0),
        "proj_weight": bell_draw(splits[6], (D, D), (D * 16 // CAP) ** -0.5, 2.0, ((0, 2),), jnp.float32),
        "proj_mean": bell_draw(splits[7], (D, D), (0.11 * (12 * (TOKENS // CAP)) ** 0.5), 4.0, ((0, 2),), jnp.float32),
        "proj_square": jnp.clip(jnp.exp(math.log(30.72) - 2.7725887 * jax.random.uniform(splits[8], (D, D), jnp.float32) ** block_scale(splits[8], (D, D), ((0, 2),), -0.2, 0.2)), 1.92, 30.72),
        "inner_weight": bell_draw(splits[9], (2, D, FF), D ** -0.5, 0.1875, ((2, 2),), jnp.float32),
        "inner_mean": bell_draw(splits[10], (2, D, FF), (0.11 * (0.1 * TOKENS) ** 0.5), 40.0, ((2, 2),), jnp.float32),
        "inner_square": jnp.clip(jnp.exp(math.log(524.288) - 2.7725887 * jax.random.uniform(splits[11], (2, D, FF), jnp.float32) ** block_scale(splits[11], (2, D, FF), ((2, 2),), -0.2, 0.2)), 32.768, 524.288),
        "down_weight": bell_draw(splits[12], (FF, D), FF ** -0.5, 0.125, ((0, 2),), jnp.float32),
        "down_mean": bell_draw(splits[13], (FF, D), (0.11 * (0.25 * TOKENS) ** 0.5), 64.0, ((0, 2),), jnp.float32),
        "down_square": jnp.clip(jnp.exp(math.log(1310.72) - 2.7725887 * jax.random.uniform(splits[14], (FF, D), jnp.float32) ** block_scale(splits[14], (FF, D), ((0, 2),), -0.2, 0.2)), 81.92, 1310.72),
        "norm_gains": jnp.clip(1.0 + 0.1 * jax.random.normal(splits[15], (2, D), jnp.float32), 0.5, 1.5),
        "gains_mean": draw_gains_mean(jax.random.fold_in(splits[18], 71), 0),
        "gains_square": draw_gains_square(jax.random.fold_in(splits[18], 71), 0),
    }


@jax.custom_vjp
def low(v):
    return lax.optimization_barrier(v.astype(jnp.bfloat16)).astype(jnp.float32)

@jax.custom_vjp
def low_back(v):
    return v

def low_keep(v):
    return (low(v), None)

def low_pass(kept, grad):
    return (grad,)

def back_keep(v):
    return (v, None)

def back_low(kept, grad):
    return (low(grad),)
low.defvjp(low_keep, low_pass)
low_back.defvjp(back_keep, back_low)
eps_norm = 1e-05
rope_base = 160000.0
beta_one = 0.9
beta_two = 0.98
adam_eps = 1e-08
decay_value = 0.01
gain_rate = 0.6

def normalize(values):
    center = values - lax.optimization_barrier(jnp.mean(values, axis=-1, keepdims=True))
    inverse = lax.rsqrt(lax.optimization_barrier(jnp.mean(center * center, axis=-1, keepdims=True)) + eps_norm)
    return center * inverse

def layout_info(lengths, row_index):
    seq_ends = jnp.cumsum(lengths)
    before = seq_ends[None, :] <= row_index[:, None]
    segment = lax.optimization_barrier(jnp.sum(before.astype(jnp.int32), axis=1))
    offset = lax.optimization_barrier(jnp.sum(jnp.where(before, lengths[None, :], 0), axis=1))
    position = (row_index - offset).astype(jnp.float32)
    live_rows = (row_index < seq_ends[-1]).astype(jnp.float32)
    return (segment, position, live_rows)

def rope_tables(position, head_dim):
    half_dim = head_dim // 2
    frequency = rope_base ** (-(2.0 * jnp.arange(half_dim, dtype=jnp.float32)) / head_dim)
    angles = position[:, None] * frequency[None, :]
    angles = jnp.concatenate([angles, angles], axis=1)
    return (jnp.cos(angles)[:, None, :], jnp.sin(angles)[:, None, :])

def rotate(values):
    half_dim = values.shape[-1] // 2
    return jnp.concatenate([-values[..., half_dim:], values[..., :half_dim]], axis=-1)

def adam_step(weight, first_old, second_old, gradient, step_rate, weight_decay):
    first_new = beta_one * first_old + (1.0 - beta_one) * gradient
    second_new = beta_two * second_old + (1.0 - beta_two) * gradient * gradient
    fix_one = 1.0 - beta_one ** STEP
    fix_two = 1.0 - beta_two ** STEP
    update = first_new / fix_one / (jnp.sqrt(second_new / fix_two) + adam_eps)
    return (first_new, second_new, weight - step_rate * (update + weight_decay * weight))

def reference(tokens, cotangent, seq_lengths, qkv_weight, qkv_mean, qkv_square, proj_weight, proj_mean, proj_square, inner_weight, inner_mean, inner_square, down_weight, down_mean, down_square, norm_gains, gains_mean, gains_square):
    highest = lax.Precision.HIGHEST
    row_index = jnp.arange(CAP, dtype=jnp.int32)
    segment, position, live = jax.vmap(lambda lengths: layout_info(lengths, row_index))(seq_lengths)

    def forward(params, resid_in):
        qkv_w, proj_w, inner_w, down_w, gains_w = params
        qkv_low = low(qkv_w)
        proj_low = low(proj_w)
        inner_low = low(inner_w)
        down_low = low(down_w)
        gain_low = low(gains_w)
        inputs_dev = resid_in.reshape(N_DP, CAP, D)

        def one_device(pieces):
            values, seg_ids, pos_vals, live_rows = pieces
            attn_hat = normalize(values)
            attn_in = low(attn_hat * gain_low[0])
            qkv_raw = low_back(jnp.einsum('td,kdf->ktf', attn_in, qkv_low, precision=highest))
            cosine, sine_table = rope_tables(pos_vals, HEAD_DIM)
            query_raw = qkv_raw[0].reshape(CAP, HEADS, HEAD_DIM)
            key_raw = qkv_raw[1].reshape(CAP, HEADS, HEAD_DIM)
            query_all = low(query_raw * cosine + rotate(query_raw) * sine_table)
            key_all = low(key_raw * cosine + rotate(key_raw) * sine_table)
            value_all = low(qkv_raw[2].reshape(CAP, HEADS, HEAD_DIM))
            allowed = seg_ids[:, None] == seg_ids[None, :]

            def one_head(head_parts):
                query_head, key_head, value_head = head_parts
                scores = low_back(jnp.dot(query_head, key_head.T, precision=highest) * 0.125)
                scores = jnp.where(allowed, scores, -1e+30)
                row_peak = lax.optimization_barrier(jnp.max(scores, axis=-1, keepdims=True))
                exponent = jnp.exp(scores - row_peak)
                prob_block = exponent / lax.optimization_barrier(jnp.sum(exponent, axis=-1, keepdims=True))
                mixture = jnp.dot(low(prob_block), value_head, precision=highest)
                return low(low_back(mixture))
            heads_out = lax.map(jax.checkpoint(one_head), (jnp.transpose(query_all, (1, 0, 2)), jnp.transpose(key_all, (1, 0, 2)), jnp.transpose(value_all, (1, 0, 2))))
            attn_out = jnp.transpose(heads_out, (1, 0, 2)).reshape(CAP, D)
            resid_mid = values + low_back(jnp.dot(attn_out, proj_low, precision=highest))
            mlp_hat = normalize(resid_mid)
            mlp_in = low(mlp_hat * gain_low[1])
            gate_up = low_back(jnp.einsum('td,kdf->ktf', mlp_in, inner_low, precision=highest))
            hidden = low(jax.nn.gelu(gate_up[0], approximate=False) * gate_up[1])
            resid_out = resid_mid + low_back(jnp.dot(hidden, down_low, precision=highest))
            return live_rows[:, None] * resid_out
        outputs = lax.map(jax.checkpoint(one_device), (inputs_dev, segment, position, live))
        return outputs.reshape(TOKENS, D)
    params = (qkv_weight, proj_weight, inner_weight, down_weight, norm_gains)
    resid_in = tokens.astype(jnp.float32)
    result, pullback = jax.vjp(forward, params, resid_in)
    weight_grads, input_grad = pullback(cotangent.astype(jnp.float32))
    qkv_grad, proj_grad, inner_grad, down_grad, gain_grad = weight_grads
    layer_out = result.astype(jnp.bfloat16)
    qkv_first, qkv_second, qkv_updated = adam_step(qkv_weight, qkv_mean, qkv_square, qkv_grad, float(D) ** (-0.5), decay_value)
    proj_first, proj_second, proj_updated = adam_step(proj_weight, proj_mean, proj_square, proj_grad, float(D * 16 // CAP) ** (-0.5), decay_value)
    inner_first, inner_second, inner_updated = adam_step(inner_weight, inner_mean, inner_square, inner_grad, float(D) ** (-0.5), decay_value)
    down_first, down_second, down_updated = adam_step(down_weight, down_mean, down_square, down_grad, float(FF) ** (-0.5), decay_value)
    gains_first, gains_second, gains_updated = adam_step(norm_gains, gains_mean, gains_square, gain_grad, gain_rate, 0.0)
    return (layer_out, input_grad, qkv_first, qkv_second, qkv_updated, proj_first, proj_second, proj_updated, inner_first, inner_second, inner_updated, down_first, down_second, down_updated, gains_first, gains_second, gains_updated)
```

```python
import functools

import jax
import jax.numpy as jnp
from jax import lax
from jax.experimental import pallas as pl
from jax.experimental.pallas import tpu as pltpu
from jax.sharding import PartitionSpec as P

D = 1024
HEAD_DIM = 64
FF = 2624
CAP = 2048
STEP = 10


eps_norm = 1e-05
rope_base = 160000.0
beta_one = 0.9
beta_two = 0.98
adam_eps = 1e-08
decay_value = 0.01
gain_rate = 0.6
sqrt_half = 0.7071067811865476
inv_sqrt_tau = 0.3989422804014327


def normalize(values):
    center = values - jnp.mean(values, axis=-1, keepdims=True)
    inverse = lax.rsqrt(jnp.mean(center * center, axis=-1, keepdims=True) + eps_norm)
    return (center * inverse, inverse)


def norm_back(upstream, normed, inverse, gain_row):
    weighted = upstream * gain_row
    row_inner = jnp.mean(weighted * normed, axis=-1, keepdims=True)
    grad_in = inverse * (weighted - jnp.mean(weighted, axis=-1, keepdims=True) - normed * row_inner)
    return grad_in


def layout_info(seq_lengths, row_index):
    lengths = seq_lengths.reshape(-1)
    seq_ends = jnp.cumsum(lengths)
    before = seq_ends[None, :] <= row_index[:, None]
    segment = jnp.sum(before.astype(jnp.int32), axis=1)
    offset = jnp.sum(jnp.where(before, lengths[None, :], 0), axis=1)
    position = (row_index - offset).astype(jnp.float32)
    live_rows = (row_index < seq_ends[-1]).astype(jnp.float32)
    return (segment, position, live_rows)


def rope_tables(position):
    half_dim = HEAD_DIM // 2
    frequency = rope_base ** (-(2.0 * jnp.arange(half_dim, dtype=jnp.float32)) / HEAD_DIM)
    angles = position[:, None] * frequency[None, :]
    return (jnp.tile(jnp.cos(angles), (1, 4)), jnp.tile(jnp.sin(angles), (1, 4)))


def gelu_parts(values):
    normal_cdf = 0.5 * (1.0 + lax.erf(values * sqrt_half))
    density = inv_sqrt_tau * jnp.exp(-0.5 * values * values)
    return (values * normal_cdf, normal_cdf + values * density)


def adam_step(weight, first_old, second_old, gradient, step_rate, weight_decay):
    first_new = beta_one * first_old + (1.0 - beta_one) * gradient
    second_new = beta_two * second_old + (1.0 - beta_two) * gradient * gradient
    fix_one = 1.0 - beta_one**STEP
    fix_two = 1.0 - beta_two**STEP
    update = first_new / fix_one / (jnp.sqrt(second_new / fix_two) + adam_eps)
    return (first_new, second_new, weight - step_rate * (update + weight_decay * weight))


def contract_rows(left, right):
    return lax.dot_general(
        left, right, (((0,), (0,)), ((), ())), preferred_element_type=jnp.float32
    )


def contract_cols(left, right):
    return lax.dot_general(
        left, right, (((1,), (1,)), ((), ())), preferred_element_type=jnp.float32
    )


VMEM_LIMIT = 56 * 1024 * 1024
PAIR = 2 * HEAD_DIM


def rotate_pair(values):
    lane = lax.broadcasted_iota(jnp.int32, values.shape, 1)
    first_half = lane % HEAD_DIM < HEAD_DIM // 2
    return jnp.where(
        first_half, -pltpu.roll(values, PAIR - HEAD_DIM // 2, 1), pltpu.roll(values, HEAD_DIM // 2, 1)
    )


def split_heads(values):
    lane = lax.broadcasted_iota(jnp.int32, values.shape, 1)
    zero = jnp.zeros_like(values)
    return (
        jnp.where(lane < HEAD_DIM, values, zero),
        jnp.where(lane >= HEAD_DIM, values, zero),
    )


def forward_kernel(rows, seg_ref, raw_ref, cos_ref, sin_ref, col_ref, row_ref, low_ref, out_ref, lse_ref):
    step = pl.program_id(1)
    total = raw_ref.shape[1]
    half = total // 2

    @pl.when(step == 0)
    def _():
        key_raw = raw_ref[1]
        low_ref[1] = (key_raw * cos_ref[...] + rotate_pair(key_raw) * sin_ref[...]).astype(jnp.bfloat16)
        low_ref[2] = raw_ref[2].astype(jnp.bfloat16)

    here = pl.ds(pl.multiple_of(step * rows, rows), rows)
    query_raw = raw_ref[0, here, :]
    query = (query_raw * cos_ref[here, :] + rotate_pair(query_raw) * sin_ref[here, :]).astype(jnp.bfloat16)
    query = query * jnp.bfloat16(0.125)
    low_ref[0, here, :] = query
    first = seg_ref[0]
    single = (first == seg_ref[half - 1]) & (first == seg_ref[half]) & (first == seg_ref[total - 1])

    def work(masked):
        outs, logs = [], []
        for part in split_heads(query):
            scores = contract_cols(part, low_ref[1])
            if masked:
                scores = jnp.where(col_ref[here, :1] == row_ref[:1, :], scores, -1e30)
            peak = jnp.max(scores, axis=1, keepdims=True)
            weight = jnp.exp(scores - peak)
            norm = jnp.sum(weight, axis=1, keepdims=True)
            mixed = jnp.dot(weight.astype(jnp.bfloat16), low_ref[2], preferred_element_type=jnp.float32)
            outs.append(mixed / norm)
            logs.append(peak + jnp.log(norm))
        lane = lax.broadcasted_iota(jnp.int32, (rows, PAIR), 1)
        out_ref[...] = jnp.where(lane < HEAD_DIM, outs[0], outs[1]).astype(jnp.bfloat16)
        both = jnp.where(lane == 0, logs[0], logs[1])
        lse_ref[0] = jnp.transpose(both)[:8]

    pl.when(single)(lambda: work(False))
    pl.when(jnp.logical_not(single))(lambda: work(True))


def attention_forward(raw, cosine, sine, segment):
    _, total, width = raw.shape
    rows = min(256, total)
    pairs = width // PAIR
    column = jnp.broadcast_to(segment[:, None], (total, PAIR))
    line = jnp.broadcast_to(segment[None, :], (8, total))
    whole = lambda p, i, s: (0, 0)
    return pl.pallas_call(
        functools.partial(forward_kernel, rows),
        grid_spec=pltpu.PrefetchScalarGridSpec(
            num_scalar_prefetch=1,
            grid=(pairs, total // rows),
            in_specs=[
                pl.BlockSpec((3, total, PAIR), lambda p, i, s: (0, 0, p)),
                pl.BlockSpec((total, PAIR), whole),
                pl.BlockSpec((total, PAIR), whole),
                pl.BlockSpec((total, PAIR), whole),
                pl.BlockSpec((8, total), whole),
            ],
            out_specs=[
                pl.BlockSpec((3, total, PAIR), lambda p, i, s: (0, 0, p)),
                pl.BlockSpec((rows, PAIR), lambda p, i, s: (i, p)),
                pl.BlockSpec((1, 8, rows), lambda p, i, s: (p, 0, i)),
            ],
        ),
        out_shape=[
            jax.ShapeDtypeStruct((3, total, width), jnp.bfloat16),
            jax.ShapeDtypeStruct((total, width), jnp.bfloat16),
            jax.ShapeDtypeStruct((pairs, 8, total), jnp.float32),
        ],
        compiler_params=pltpu.CompilerParams(vmem_limit_bytes=VMEM_LIMIT),
        cost_estimate=pl.CostEstimate(
            flops=16 * total * total * width, bytes_accessed=20 * total * width, transcendentals=0
        ),
    )(segment, raw, cosine, sine, column, line)


def backward_kernel(
    rows, chunk, seg_ref, low_ref, grad_ref, out_ref, lse_ref, cos_ref, sin_ref, col_ref, row_ref,
    result_ref, key_acc, value_acc, query_acc,
):
    step = pl.program_id(1)
    total = low_ref.shape[1]

    @pl.when(step == 0)
    def _():
        key_acc[...] = jnp.zeros_like(key_acc)
        value_acc[...] = jnp.zeros_like(value_acc)

    here = pl.ds(pl.multiple_of(step * rows, rows), rows)
    query = jnp.concatenate(split_heads(low_ref[0, here, :]), axis=0)
    grad_now = grad_ref[...]
    grad = jnp.concatenate(split_heads(grad_now), axis=0)
    product = jnp.transpose(grad_now.astype(jnp.float32) * out_ref[...].astype(jnp.float32))
    inner = jnp.concatenate(
        [
            jnp.sum(product[:HEAD_DIM], axis=0, keepdims=True),
            jnp.sum(product[HEAD_DIM:], axis=0, keepdims=True),
        ],
        axis=1,
    )
    log_total = jnp.concatenate([lse_ref[0, 0:1, :], lse_ref[0, 1:2, :]], axis=1)
    line = jnp.concatenate([row_ref[:1, :], row_ref[:1, :]], axis=1)
    query_acc[...] = jnp.zeros_like(query_acc)
    query_first, query_last = seg_ref[step * rows], seg_ref[step * rows + rows - 1]

    def work(at, masked):
        there = pl.ds(pl.multiple_of(at * chunk, chunk), chunk)
        key, value = low_ref[1, there, :], low_ref[2, there, :]
        scores = contract_cols(key, query)
        if masked:
            scores = jnp.where(col_ref[there, :1] == line, scores, -1e30)
        prob = jnp.exp(scores - log_total)
        grad_prob = contract_cols(value, grad)
        grad_scores = (prob * (grad_prob - inner)).astype(jnp.bfloat16)
        value_acc[there, :] += jnp.dot(prob.astype(jnp.bfloat16), grad, preferred_element_type=jnp.float32)
        key_acc[there, :] += jnp.dot(grad_scores, query, preferred_element_type=jnp.float32)
        query_acc[...] += contract_rows(grad_scores, key)

    def visit(at, carry):
        key_first, key_last = seg_ref[at * chunk], seg_ref[at * chunk + chunk - 1]
        meets = (key_first <= query_last) & (query_first <= key_last)
        single = (key_first == key_last) & (query_first == query_last)
        pl.when(meets & single)(lambda: work(at, False))
        pl.when(meets & jnp.logical_not(single))(lambda: work(at, True))
        return carry

    lax.fori_loop(0, total // chunk, visit, 0)
    lane = lax.broadcasted_iota(jnp.int32, (rows, PAIR), 1)
    grad_query = 0.125 * jnp.where(lane < HEAD_DIM, query_acc[:rows, :], query_acc[rows:, :])
    result_ref[0, here, :] = (
        grad_query * cos_ref[here, :] - rotate_pair(grad_query * sin_ref[here, :])
    ).astype(jnp.bfloat16)

    @pl.when(step == pl.num_programs(1) - 1)
    def _():
        grad_key = key_acc[...]
        result_ref[1] = (grad_key * cos_ref[...] - rotate_pair(grad_key * sin_ref[...])).astype(jnp.bfloat16)
        result_ref[2] = value_acc[...].astype(jnp.bfloat16)


def attention_backward(low, grad, out, log_total, cosine, sine, segment):
    _, total, width = low.shape
    rows = min(256, total)
    chunk = min(1024, total // 2)
    pairs = width // PAIR
    column = jnp.broadcast_to(segment[:, None], (total, PAIR))
    line = jnp.broadcast_to(segment[None, :], (8, total))
    whole = lambda p, i, s: (0, 0)
    return pl.pallas_call(
        functools.partial(backward_kernel, rows, chunk),
        grid_spec=pltpu.PrefetchScalarGridSpec(
            num_scalar_prefetch=1,
            grid=(pairs, total // rows),
            in_specs=[
                pl.BlockSpec((3, total, PAIR), lambda p, i, s: (0, 0, p)),
                pl.BlockSpec((rows, PAIR), lambda p, i, s: (i, p)),
                pl.BlockSpec((rows, PAIR), lambda p, i, s: (i, p)),
                pl.BlockSpec((1, 8, rows), lambda p, i, s: (p, 0, i)),
                pl.BlockSpec((total, PAIR), whole),
                pl.BlockSpec((total, PAIR), whole),
                pl.BlockSpec((total, PAIR), whole),
                pl.BlockSpec((8, rows), lambda p, i, s: (0, i)),
            ],
            out_specs=pl.BlockSpec((3, total, PAIR), lambda p, i, s: (0, 0, p)),
            scratch_shapes=[
                pltpu.VMEM((total, PAIR), jnp.float32),
                pltpu.VMEM((total, PAIR), jnp.float32),
                pltpu.VMEM((2 * rows, PAIR), jnp.float32),
            ],
        ),
        out_shape=jax.ShapeDtypeStruct((3, total, width), jnp.bfloat16),
        compiler_params=pltpu.CompilerParams(vmem_limit_bytes=VMEM_LIMIT),
        cost_estimate=pl.CostEstimate(
            flops=40 * total * total * width, bytes_accessed=16 * total * width, transcendentals=0
        ),
    )(segment, low, grad, out, log_total, cosine, sine, column, line)


SWAP = ((0, 1), (1, 0))


def gather_rows(own):
    if lax.axis_size("tensor") == 2:
        return jnp.concatenate([own, lax.ppermute(own, "tensor", SWAP)], axis=0)
    return lax.all_gather(own, "tensor", axis=0, tiled=True)


def scatter_rows(product, left):
    if lax.axis_size("tensor") == 2:
        half = left.shape[-2] // 2
        sent = product(left[..., half:, :]).astype(jnp.bfloat16)
        arrived = lax.ppermute(sent, "tensor", SWAP)
        return product(left[..., :half, :]) + arrived.astype(jnp.float32)
    return lax.psum_scatter(
        product(left).astype(jnp.bfloat16), "tensor", scatter_dimension=0, tiled=True
    ).astype(jnp.float32)


def sum_tensor(values):
    if lax.axis_size("tensor") == 2:
        return values + lax.ppermute(values, "tensor", SWAP)
    return lax.psum(values, "tensor")


def shards(
    tokens,
    cotangent,
    seq_lengths,
    qkv_weight,
    qkv_mean,
    qkv_square,
    proj_weight,
    proj_mean,
    proj_square,
    inner_weight,
    inner_mean,
    inner_square,
    down_weight,
    down_mean,
    down_square,
    norm_gains,
    gains_mean,
    gains_square,
):
    groups = lax.axis_size("tensor")
    row_count = tokens.shape[0]
    capacity = row_count * groups
    all_rows = jnp.arange(capacity, dtype=jnp.int32)
    first_row = lax.axis_index("tensor") * row_count
    if groups == 2:
        all_rows = jnp.where(all_rows < row_count, all_rows + first_row, all_rows - first_row)
    segment, position, live_all = layout_info(seq_lengths, all_rows)
    own_rows = first_row + jnp.arange(row_count, dtype=jnp.int32)
    live_own = layout_info(seq_lengths, own_rows)[2][:, None]
    qkv_low = qkv_weight.astype(jnp.bfloat16)
    proj_low = proj_weight.astype(jnp.bfloat16)
    inner_low = inner_weight.astype(jnp.bfloat16)
    down_low = down_weight.astype(jnp.bfloat16)
    gain_low = lax.optimization_barrier(norm_gains.astype(jnp.bfloat16)).astype(jnp.float32)
    cosine, sine = rope_tables(position)
    resid_in = tokens.astype(jnp.float32)
    attn_hat, attn_inv = normalize(resid_in)
    attn_in = (attn_hat * gain_low[0]).astype(jnp.bfloat16)
    attn_full = gather_rows(attn_in)
    grad_out = cotangent.astype(jnp.float32) * live_own
    grad_low, attn_full = lax.optimization_barrier((grad_out.astype(jnp.bfloat16), attn_full))
    grad_full = gather_rows(grad_low)
    qkv_raw = jnp.einsum("td,kdf->ktf", attn_full, qkv_low, preferred_element_type=jnp.float32)
    attn_parts, attn_low, log_total = attention_forward(qkv_raw, cosine, sine, segment)
    resid_mid = resid_in + scatter_rows(
        lambda left: jnp.dot(left, proj_low, preferred_element_type=jnp.float32), attn_low
    )
    mlp_hat, mlp_inv = normalize(resid_mid)
    mlp_in = (mlp_hat * gain_low[1]).astype(jnp.bfloat16)
    mlp_full = gather_rows(mlp_in)
    grad_hidden = contract_cols(grad_full, down_low)
    gate = jnp.dot(mlp_full, inner_low[0], preferred_element_type=jnp.float32)
    up = jnp.dot(mlp_full, inner_low[1], preferred_element_type=jnp.float32)
    gelu_val, gelu_slope = gelu_parts(gate)
    hidden_low = (gelu_val * up).astype(jnp.bfloat16)
    grad_gate = (grad_hidden * up * gelu_slope).astype(jnp.bfloat16)
    grad_up = (grad_hidden * gelu_val).astype(jnp.bfloat16)
    grad_norm = scatter_rows(
        lambda left: contract_cols(left[0], inner_low[0]) + contract_cols(left[1], inner_low[1]),
        jnp.stack([grad_gate, grad_up]),
    )
    inner_grad = jnp.stack([contract_rows(mlp_full, grad_gate), contract_rows(mlp_full, grad_up)])
    down_grad = contract_rows(hidden_low, grad_full)
    inner_sum = lax.psum(inner_grad.astype(jnp.bfloat16), "dp")
    down_sum = lax.psum(down_grad.astype(jnp.bfloat16), "dp")
    grad_mid = grad_out + norm_back(grad_norm, mlp_hat, mlp_inv, gain_low[1])
    grad_mid_full = gather_rows(grad_mid.astype(jnp.bfloat16))
    grad_attn = contract_cols(grad_mid_full, proj_low).astype(jnp.bfloat16)
    hidden_late, grad_attn = lax.optimization_barrier((hidden_low, grad_attn))
    resid_out = resid_mid + scatter_rows(
        lambda left: jnp.dot(left, down_low, preferred_element_type=jnp.float32), hidden_late
    )
    layer_out = (live_own * resid_out).astype(jnp.bfloat16)
    grad_qkv = attention_backward(
        attn_parts, grad_attn, attn_low, log_total, cosine, sine, segment
    )
    proj_grad = contract_rows(attn_low, grad_mid_full)
    grad_qkv, inner_sum, down_sum = lax.optimization_barrier((grad_qkv, inner_sum, down_sum))
    qkv_grad = jnp.stack([contract_rows(attn_full, grad_qkv[k]) for k in range(3)])
    qkv_sum = lax.psum(qkv_grad.astype(jnp.bfloat16), "dp")
    proj_grad, down_sum = lax.optimization_barrier((proj_grad, down_sum))
    proj_sum = lax.psum(proj_grad.astype(jnp.bfloat16), "dp")
    grad_attn_norm = scatter_rows(
        lambda left: sum(contract_cols(left[k], qkv_low[k]) for k in range(3)), grad_qkv
    )
    input_grad = grad_mid + norm_back(grad_attn_norm, attn_hat, attn_inv, gain_low[0])
    qkv_grad, proj_grad, inner_grad, down_grad = (
        qkv_sum.astype(jnp.float32),
        proj_sum.astype(jnp.float32),
        inner_sum.astype(jnp.float32),
        down_sum.astype(jnp.float32),
    )
    gain_grad = sum_tensor(
        jnp.stack(
            [
                jnp.sum(qkv_grad * qkv_low.astype(jnp.float32), axis=(0, 2)),
                jnp.sum(inner_grad * inner_low.astype(jnp.float32), axis=(0, 2)),
            ]
        )
    ) / gain_low
    qkv_first, qkv_second, qkv_updated = adam_step(
        qkv_weight, qkv_mean, qkv_square, qkv_grad, float(D) ** (-0.5), decay_value
    )
    proj_first, proj_second, proj_updated = adam_step(
        proj_weight, proj_mean, proj_square, proj_grad, float(D * 16 // CAP) ** (-0.5), decay_value
    )
    inner_first, inner_second, inner_updated = adam_step(
        inner_weight, inner_mean, inner_square, inner_grad, float(D) ** (-0.5), decay_value
    )
    down_first, down_second, down_updated = adam_step(
        down_weight, down_mean, down_square, down_grad, float(FF) ** (-0.5), decay_value
    )
    gains_first, gains_second, gains_updated = adam_step(
        norm_gains, gains_mean, gains_square, gain_grad, gain_rate, 0.0
    )
    return (
        layer_out,
        input_grad,
        qkv_first,
        qkv_second,
        qkv_updated,
        proj_first,
        proj_second,
        proj_updated,
        inner_first,
        inner_second,
        inner_updated,
        down_first,
        down_second,
        down_updated,
        gains_first,
        gains_second,
        gains_updated,
    )


def solution(mesh):
    in_specs = (
        P(("dp", "tensor"), None),
        P(("dp", "tensor"), None),
        P("dp", None),
        P(None, None, "tensor"),
        P(None, None, "tensor"),
        P(None, None, "tensor"),
        P("tensor", None),
        P("tensor", None),
        P("tensor", None),
        P(None, None, "tensor"),
        P(None, None, "tensor"),
        P(None, None, "tensor"),
        P("tensor", None),
        P("tensor", None),
        P("tensor", None),
        P(),
        P(),
        P(),
    )
    out_specs = (
        P(("dp", "tensor"), None),
        P(("dp", "tensor"), None),
        P(None, None, "tensor"),
        P(None, None, "tensor"),
        P(None, None, "tensor"),
        P("tensor", None),
        P("tensor", None),
        P("tensor", None),
        P(None, None, "tensor"),
        P(None, None, "tensor"),
        P(None, None, "tensor"),
        P("tensor", None),
        P("tensor", None),
        P("tensor", None),
        P(),
        P(),
        P(),
    )
    return jax.shard_map(shards, mesh=mesh, in_specs=in_specs, out_specs=out_specs, check_vma=False)
```

```python
import functools

import jax
import jax.numpy as jnp
from jax import lax
from jax.experimental import pallas as pl
from jax.experimental.pallas import tpu as pltpu
from jax.sharding import PartitionSpec as P

D = 1024
HEAD_DIM = 64
FF = 2624
CAP = 2048
STEP = 10


eps_norm = 1e-05
rope_base = 160000.0
beta_one = 0.9
beta_two = 0.98
adam_eps = 1e-08
decay_value = 0.01
gain_rate = 0.6
sqrt_half = 0.7071067811865476
inv_sqrt_tau = 0.3989422804014327


def normalize(values):
    center = values - jnp.mean(values, axis=-1, keepdims=True)
    inverse = lax.rsqrt(jnp.mean(center * center, axis=-1, keepdims=True) + eps_norm)
    return (center * inverse, inverse)


def norm_back(upstream, normed, inverse, gain_row):
    weighted = upstream * gain_row
    row_inner = jnp.mean(weighted * normed, axis=-1, keepdims=True)
    grad_in = inverse * (weighted - jnp.mean(weighted, axis=-1, keepdims=True) - normed * row_inner)
    return grad_in


def layout_info(seq_lengths, row_index):
    lengths = seq_lengths.reshape(-1)
    seq_ends = jnp.cumsum(lengths)
    before = seq_ends[None, :] <= row_index[:, None]
    segment = jnp.sum(before.astype(jnp.int32), axis=1)
    offset = jnp.sum(jnp.where(before, lengths[None, :], 0), axis=1)
    position = (row_index - offset).astype(jnp.float32)
    live_rows = (row_index < seq_ends[-1]).astype(jnp.float32)
    return (segment, position, live_rows)


def rope_tables(position):
    half_dim = HEAD_DIM // 2
    frequency = rope_base ** (-(2.0 * jnp.arange(half_dim, dtype=jnp.float32)) / HEAD_DIM)
    angles = position[:, None] * frequency[None, :]
    return (jnp.tile(jnp.cos(angles), (1, 4)), jnp.tile(jnp.sin(angles), (1, 4)))


def gelu_parts(values):
    normal_cdf = 0.5 * (1.0 + lax.erf(values * sqrt_half))
    density = inv_sqrt_tau * jnp.exp(-0.5 * values * values)
    return (values * normal_cdf, normal_cdf + values * density)


def adam_step(weight, first_old, second_old, gradient, step_rate, weight_decay):
    first_new = beta_one * first_old + (1.0 - beta_one) * gradient
    second_new = beta_two * second_old + (1.0 - beta_two) * gradient * gradient
    fix_one = 1.0 - beta_one**STEP
    fix_two = 1.0 - beta_two**STEP
    update = first_new / fix_one / (jnp.sqrt(second_new / fix_two) + adam_eps)
    return (first_new, second_new, weight - step_rate * (update + weight_decay * weight))


def contract_rows(left, right):
    return lax.dot_general(
        left, right, (((0,), (0,)), ((), ())), preferred_element_type=jnp.float32
    )


def contract_cols(left, right):
    return lax.dot_general(
        left, right, (((1,), (1,)), ((), ())), preferred_element_type=jnp.float32
    )


VMEM_LIMIT = 56 * 1024 * 1024
PAIR = 2 * HEAD_DIM


def rotate_pair(values):
    lane = lax.broadcasted_iota(jnp.int32, values.shape, 1)
    first_half = lane % HEAD_DIM < HEAD_DIM // 2
    return jnp.where(
        first_half, -pltpu.roll(values, PAIR - HEAD_DIM // 2, 1), pltpu.roll(values, HEAD_DIM // 2, 1)
    )


def split_heads(values):
    lane = lax.broadcasted_iota(jnp.int32, values.shape, 1)
    zero = jnp.zeros_like(values)
    return (
        jnp.where(lane < HEAD_DIM, values, zero),
        jnp.where(lane >= HEAD_DIM, values, zero),
    )


def forward_kernel(rows, offset, seg_ref, raw_ref, cos_ref, sin_ref, col_ref, row_ref, low_ref, out_ref, lse_ref):
    step = pl.program_id(1)
    total = raw_ref.shape[1]
    half = total // 2

    @pl.when(step == 0)
    def _():
        key_raw = raw_ref[1]
        low_ref[1] = (key_raw * cos_ref[...] + rotate_pair(key_raw) * sin_ref[...]).astype(jnp.bfloat16)
        low_ref[2] = raw_ref[2].astype(jnp.bfloat16)
        query_raw = raw_ref[0]
        query_all = (query_raw * cos_ref[...] + rotate_pair(query_raw) * sin_ref[...]).astype(jnp.bfloat16)
        low_ref[0] = query_all * jnp.bfloat16(0.125)

    here = pl.ds(pl.multiple_of(offset + step * rows, rows), rows)
    query = low_ref[0, here, :]
    first = seg_ref[0]
    single = (first == seg_ref[half - 1]) & (first == seg_ref[half]) & (first == seg_ref[total - 1])

    def work(masked):
        outs, logs = [], []
        for part in split_heads(query):
            scores = contract_cols(part, low_ref[1])
            if masked:
                scores = jnp.where(col_ref[here, :1] == row_ref[:1, :], scores, -1e30)
            peak = jnp.max(scores, axis=1, keepdims=True)
            weight = jnp.exp(scores - peak)
            norm = jnp.sum(weight, axis=1, keepdims=True)
            mixed = jnp.dot(weight.astype(jnp.bfloat16), low_ref[2], preferred_element_type=jnp.float32)
            outs.append(mixed / norm)
            logs.append(peak + jnp.log(norm))
        lane = lax.broadcasted_iota(jnp.int32, (rows, PAIR), 1)
        out_ref[...] = jnp.where(lane < HEAD_DIM, outs[0], outs[1]).astype(jnp.bfloat16)
        both = jnp.where(lane == 0, logs[0], logs[1])
        lse_ref[0] = jnp.transpose(both)[:8]

    pl.when(single)(lambda: work(False))
    pl.when(jnp.logical_not(single))(lambda: work(True))


def attention_forward(raw, cosine, sine, segment, offset, count):
    _, total, width = raw.shape
    rows = min(256, count)
    pairs = width // PAIR
    column = jnp.broadcast_to(segment[:, None], (total, PAIR))
    line = jnp.broadcast_to(segment[None, :], (8, total))
    whole = lambda p, i, s: (0, 0)
    return pl.pallas_call(
        functools.partial(forward_kernel, rows, offset),
        grid_spec=pltpu.PrefetchScalarGridSpec(
            num_scalar_prefetch=1,
            grid=(pairs, count // rows),
            in_specs=[
                pl.BlockSpec((3, total, PAIR), lambda p, i, s: (0, 0, p)),
                pl.BlockSpec((total, PAIR), whole),
                pl.BlockSpec((total, PAIR), whole),
                pl.BlockSpec((total, PAIR), whole),
                pl.BlockSpec((8, total), whole),
            ],
            out_specs=[
                pl.BlockSpec((3, total, PAIR), lambda p, i, s: (0, 0, p)),
                pl.BlockSpec((rows, PAIR), lambda p, i, s: (i, p)),
                pl.BlockSpec((1, 8, rows), lambda p, i, s: (p, 0, i)),
            ],
        ),
        out_shape=[
            jax.ShapeDtypeStruct((3, total, width), jnp.bfloat16),
            jax.ShapeDtypeStruct((count, width), jnp.bfloat16),
            jax.ShapeDtypeStruct((pairs, 8, count), jnp.float32),
        ],
        compiler_params=pltpu.CompilerParams(vmem_limit_bytes=VMEM_LIMIT),
        cost_estimate=pl.CostEstimate(
            flops=44 * total * count * width, bytes_accessed=20 * total * width, transcendentals=0
        ),
    )(segment, raw, cosine, sine, column, line)


def backward_kernel(
    rows, chunk, offset, last, seg_ref, low_ref, grad_ref, out_ref, lse_ref, cos_ref, sin_ref, col_ref,
    row_ref, *others,
):
    *given, query_ref, pair_ref, key_acc, value_acc, query_acc = others
    step = pl.program_id(1)
    total = low_ref.shape[1]

    @pl.when(step == 0)
    def _():
        key_acc[...] = given[0][0] if given else jnp.zeros_like(key_acc)
        value_acc[...] = given[0][1] if given else jnp.zeros_like(value_acc)

    start = offset + step * rows
    here = pl.ds(pl.multiple_of(start, rows), rows)
    query = jnp.concatenate(split_heads(low_ref[0, here, :]), axis=0)
    grad_now = grad_ref[...]
    grad = jnp.concatenate(split_heads(grad_now), axis=0)
    product = jnp.transpose(grad_now.astype(jnp.float32) * out_ref[...].astype(jnp.float32))
    inner = jnp.concatenate(
        [
            jnp.sum(product[:HEAD_DIM], axis=0, keepdims=True),
            jnp.sum(product[HEAD_DIM:], axis=0, keepdims=True),
        ],
        axis=1,
    )
    log_total = jnp.concatenate([lse_ref[0, 0:1, :], lse_ref[0, 1:2, :]], axis=1)
    line = jnp.concatenate([row_ref[:1, :], row_ref[:1, :]], axis=1)
    query_acc[...] = jnp.zeros_like(query_acc)
    query_first, query_last = seg_ref[start], seg_ref[start + rows - 1]

    def work(at, masked):
        there = pl.ds(pl.multiple_of(at * chunk, chunk), chunk)
        key, value = low_ref[1, there, :], low_ref[2, there, :]
        scores = contract_cols(key, query)
        if masked:
            scores = jnp.where(col_ref[there, :1] == line, scores, -1e30)
        prob = jnp.exp(scores - log_total)
        grad_prob = contract_cols(value, grad)
        grad_scores = (prob * (grad_prob - inner)).astype(jnp.bfloat16)
        value_acc[there, :] += jnp.dot(prob.astype(jnp.bfloat16), grad, preferred_element_type=jnp.float32)
        key_acc[there, :] += jnp.dot(grad_scores, query, preferred_element_type=jnp.float32)
        query_acc[...] += contract_rows(grad_scores, key)

    def visit(at, carry):
        key_first, key_last = seg_ref[at * chunk], seg_ref[at * chunk + chunk - 1]
        meets = (key_first <= query_last) & (query_first <= key_last)
        single = (key_first == key_last) & (query_first == query_last)
        pl.when(meets & single)(lambda: work(at, False))
        pl.when(meets & jnp.logical_not(single))(lambda: work(at, True))
        return carry

    lax.fori_loop(0, total // chunk, visit, 0)
    lane = lax.broadcasted_iota(jnp.int32, (rows, PAIR), 1)
    grad_query = 0.125 * jnp.where(lane < HEAD_DIM, query_acc[:rows, :], query_acc[rows:, :])
    query_ref[...] = (
        grad_query * cos_ref[here, :] - rotate_pair(grad_query * sin_ref[here, :])
    ).astype(jnp.bfloat16)

    @pl.when(step == pl.num_programs(1) - 1)
    def _():
        grad_key = key_acc[...]
        if last:
            grad_key = grad_key * cos_ref[...] - rotate_pair(grad_key * sin_ref[...])
        pair_ref[0] = grad_key.astype(pair_ref.dtype)
        pair_ref[1] = value_acc[...].astype(pair_ref.dtype)


def attention_backward(low, grad, out, log_total, cosine, sine, segment, offset, given, last):
    _, total, width = low.shape
    count = grad.shape[0]
    rows = min(256, count)
    skip = offset // rows
    pair_block = pl.BlockSpec((2, total, PAIR), lambda p, i, s: (0, 0, p))
    chunk = min(1024, total // 2)
    pairs = width // PAIR
    column = jnp.broadcast_to(segment[:, None], (total, PAIR))
    line = jnp.broadcast_to(segment[None, :], (8, total))
    whole = lambda p, i, s: (0, 0)
    return pl.pallas_call(
        functools.partial(backward_kernel, rows, chunk, offset, last),
        grid_spec=pltpu.PrefetchScalarGridSpec(
            num_scalar_prefetch=1,
            grid=(pairs, count // rows),
            in_specs=[
                pl.BlockSpec((3, total, PAIR), lambda p, i, s: (0, 0, p)),
                pl.BlockSpec((rows, PAIR), lambda p, i, s: (i, p)),
                pl.BlockSpec((rows, PAIR), lambda p, i, s: (i, p)),
                pl.BlockSpec((1, 8, rows), lambda p, i, s: (p, 0, i)),
                pl.BlockSpec((total, PAIR), whole),
                pl.BlockSpec((total, PAIR), whole),
                pl.BlockSpec((total, PAIR), whole),
                pl.BlockSpec((8, rows), lambda p, i, s: (0, i + skip)),
            ]
            + [pair_block] * len(given),
            out_specs=[pl.BlockSpec((rows, PAIR), lambda p, i, s: (i, p)), pair_block],
            scratch_shapes=[
                pltpu.VMEM((total, PAIR), jnp.float32),
                pltpu.VMEM((total, PAIR), jnp.float32),
                pltpu.VMEM((2 * rows, PAIR), jnp.float32),
            ],
        ),
        out_shape=[
            jax.ShapeDtypeStruct((count, width), jnp.bfloat16),
            jax.ShapeDtypeStruct((2, total, width), jnp.bfloat16 if last else jnp.float32),
        ],
        compiler_params=pltpu.CompilerParams(vmem_limit_bytes=VMEM_LIMIT),
        cost_estimate=pl.CostEstimate(
            flops=50 * total * count * width, bytes_accessed=16 * total * width, transcendentals=0
        ),
    )(segment, low, grad, out, log_total, cosine, sine, column, line, *given)


SWAP = ((0, 1), (1, 0))


def gather_rows(own):
    if lax.axis_size("tensor") == 2:
        return jnp.concatenate([own, lax.ppermute(own, "tensor", SWAP)], axis=0)
    return lax.all_gather(own, "tensor", axis=0, tiled=True)


def row_parts(own):
    if lax.axis_size("tensor") == 2:
        return [own, lax.ppermute(own, "tensor", SWAP)]
    return [lax.all_gather(own, "tensor", axis=0, tiled=True)]


def scatter_rows(product, parts):
    if len(parts) == 2:
        arrived = lax.ppermute(product(parts[1]).astype(jnp.bfloat16), "tensor", SWAP)
        return product(parts[0]) + arrived.astype(jnp.float32)
    return lax.psum_scatter(
        product(parts[0]).astype(jnp.bfloat16), "tensor", scatter_dimension=0, tiled=True
    ).astype(jnp.float32)


def sum_tensor(values):
    if lax.axis_size("tensor") == 2:
        return values + lax.ppermute(values, "tensor", SWAP)
    return lax.psum(values, "tensor")


def shards(
    tokens,
    cotangent,
    seq_lengths,
    qkv_weight,
    qkv_mean,
    qkv_square,
    proj_weight,
    proj_mean,
    proj_square,
    inner_weight,
    inner_mean,
    inner_square,
    down_weight,
    down_mean,
    down_square,
    norm_gains,
    gains_mean,
    gains_square,
):
    groups = lax.axis_size("tensor")
    row_count = tokens.shape[0]
    capacity = row_count * groups
    all_rows = jnp.arange(capacity, dtype=jnp.int32)
    first_row = lax.axis_index("tensor") * row_count
    if groups == 2:
        all_rows = jnp.where(all_rows < row_count, all_rows + first_row, all_rows - first_row)
    segment, position, live_all = layout_info(seq_lengths, all_rows)
    own_rows = first_row + jnp.arange(row_count, dtype=jnp.int32)
    live_own = layout_info(seq_lengths, own_rows)[2][:, None]
    qkv_low = qkv_weight.astype(jnp.bfloat16)
    proj_low = proj_weight.astype(jnp.bfloat16)
    inner_low = inner_weight.astype(jnp.bfloat16)
    down_low = down_weight.astype(jnp.bfloat16)
    gain_low = lax.optimization_barrier(norm_gains.astype(jnp.bfloat16)).astype(jnp.float32)
    cosine, sine = rope_tables(position)
    resid_in = tokens.astype(jnp.float32)
    attn_hat, attn_inv = normalize(resid_in)
    attn_in = (attn_hat * gain_low[0]).astype(jnp.bfloat16)
    attn_full = gather_rows(attn_in)
    grad_out = cotangent.astype(jnp.float32) * live_own
    grad_low, attn_full = lax.optimization_barrier((grad_out.astype(jnp.bfloat16), attn_full))
    qkv_raw = jnp.einsum("td,kdf->ktf", attn_full, qkv_low, preferred_element_type=jnp.float32)
    grad_parts = row_parts(grad_low)
    project = lambda left: jnp.dot(left, proj_low, preferred_element_type=jnp.float32)
    if groups == 2:
        attn_parts, attn_other, log_other = attention_forward(
            qkv_raw, cosine, sine, segment, row_count, row_count
        )
        attn_other, grad_parts = lax.optimization_barrier((attn_other, grad_parts))
        sent, qkv_raw = lax.optimization_barrier((project(attn_other).astype(jnp.bfloat16), qkv_raw))
        arrived = lax.ppermute(sent, "tensor", SWAP)
        _, attn_own, log_own = attention_forward(qkv_raw, cosine, sine, segment, 0, row_count)
        attn_pieces = [(attn_own, log_own), (attn_other, log_other)]
        resid_mid = resid_in + (project(attn_own) + arrived.astype(jnp.float32))
    else:
        attn_parts, attn_low, log_total = attention_forward(
            qkv_raw, cosine, sine, segment, 0, capacity
        )
        attn_pieces = [(attn_low, log_total)]
        resid_mid = resid_in + scatter_rows(project, [attn_low])
    mlp_hat, mlp_inv = normalize(resid_mid)
    mlp_in = (mlp_hat * gain_low[1]).astype(jnp.bfloat16)
    mlp_parts = row_parts(mlp_in)

    def feed_forward(rows_in, grad_in):
        grad_hidden = contract_cols(grad_in, down_low)
        gate = jnp.dot(rows_in, inner_low[0], preferred_element_type=jnp.float32)
        up = jnp.dot(rows_in, inner_low[1], preferred_element_type=jnp.float32)
        gelu_val, gelu_slope = gelu_parts(gate)
        hidden = (gelu_val * up).astype(jnp.bfloat16)
        grad_gate = (grad_hidden * up * gelu_slope).astype(jnp.bfloat16)
        return (hidden, grad_gate, (grad_hidden * gelu_val).astype(jnp.bfloat16))

    inner_parts = [feed_forward(*pieces) for pieces in zip(mlp_parts, grad_parts)]
    grad_norm = scatter_rows(
        lambda part: contract_cols(part[1], inner_low[0]) + contract_cols(part[2], inner_low[1]),
        inner_parts,
    )
    inner_grad = jnp.stack(
        [
            sum(contract_rows(rows_in, part[at]) for rows_in, part in zip(mlp_parts, inner_parts))
            for at in (1, 2)
        ]
    )
    down_grad = sum(contract_rows(part[0], grad_in) for part, grad_in in zip(inner_parts, grad_parts))
    inner_send, down_send = inner_grad.astype(jnp.bfloat16), down_grad.astype(jnp.bfloat16)
    grad_norm = lax.optimization_barrier((grad_norm, inner_send, down_send))[0]
    inner_sum = lax.psum(inner_send, "dp")
    down_sum = lax.psum(down_send, "dp")
    grad_mid = grad_out + norm_back(grad_norm, mlp_hat, mlp_inv, gain_low[1])
    mid_parts = row_parts(grad_mid.astype(jnp.bfloat16))
    low_pieces, given, offset = [], [], 0
    for at, (mid_part, (attn_part, log_part)) in enumerate(zip(mid_parts, attn_pieces)):
        last = at == len(mid_parts) - 1
        grad_attn = contract_cols(mid_part, proj_low).astype(jnp.bfloat16)
        if last:
            hidden_parts = [part[0] for part in inner_parts]
            hidden_parts, grad_attn = lax.optimization_barrier((hidden_parts, grad_attn))
        low_query, pair = attention_backward(
            attn_parts, grad_attn, attn_part, log_part, cosine, sine, segment, offset, given, last
        )
        low_pieces.append(low_query)
        given = [pair]
        offset += mid_part.shape[0]
    resid_out = resid_mid + scatter_rows(
        lambda left: jnp.dot(left, down_low, preferred_element_type=jnp.float32), hidden_parts
    )
    layer_out = (live_own * resid_out).astype(jnp.bfloat16)
    proj_grad = sum(contract_rows(piece[0], mid_part) for piece, mid_part in zip(attn_pieces, mid_parts))
    grad_qkv = [jnp.concatenate(low_pieces, axis=0), pair[0], pair[1]]
    grad_qkv, inner_sum, down_sum = lax.optimization_barrier((grad_qkv, inner_sum, down_sum))
    qkv_grad = jnp.stack([contract_rows(attn_full, grad_qkv[k]) for k in range(3)])
    qkv_sum = lax.psum(qkv_grad.astype(jnp.bfloat16), "dp")
    proj_grad, down_sum = lax.optimization_barrier((proj_grad, down_sum))
    proj_sum = lax.psum(proj_grad.astype(jnp.bfloat16), "dp")
    grad_attn_norm = scatter_rows(
        lambda left: sum(contract_cols(left[k], qkv_low[k]) for k in range(3)),
        [
            [grad[at * row_count : (at + 1) * row_count] for grad in grad_qkv]
            for at in range(2)
        ]
        if groups == 2
        else [grad_qkv],
    )
    input_grad = grad_mid + norm_back(grad_attn_norm, attn_hat, attn_inv, gain_low[0])
    qkv_sum, proj_sum, input_grad, layer_out = lax.optimization_barrier(
        (qkv_sum, proj_sum, input_grad, layer_out)
    )
    qkv_grad, proj_grad, inner_grad, down_grad = (
        qkv_sum.astype(jnp.float32),
        proj_sum.astype(jnp.float32),
        inner_sum.astype(jnp.float32),
        down_sum.astype(jnp.float32),
    )
    gain_grad = sum_tensor(
        jnp.stack(
            [
                jnp.sum(qkv_grad * qkv_low.astype(jnp.float32), axis=(0, 2)),
                jnp.sum(inner_grad * inner_low.astype(jnp.float32), axis=(0, 2)),
            ]
        )
    ) / gain_low
    qkv_first, qkv_second, qkv_updated = adam_step(
        qkv_weight, qkv_mean, qkv_square, qkv_grad, float(D) ** (-0.5), decay_value
    )
    proj_first, proj_second, proj_updated = adam_step(
        proj_weight, proj_mean, proj_square, proj_grad, float(D * 16 // CAP) ** (-0.5), decay_value
    )
    inner_first, inner_second, inner_updated = adam_step(
        inner_weight, inner_mean, inner_square, inner_grad, float(D) ** (-0.5), decay_value
    )
    down_first, down_second, down_updated = adam_step(
        down_weight, down_mean, down_square, down_grad, float(FF) ** (-0.5), decay_value
    )
    gains_first, gains_second, gains_updated = adam_step(
        norm_gains, gains_mean, gains_square, gain_grad, gain_rate, 0.0
    )
    return (
        layer_out,
        input_grad,
        qkv_first,
        qkv_second,
        qkv_updated,
        proj_first,
        proj_second,
        proj_updated,
        inner_first,
        inner_second,
        inner_updated,
        down_first,
        down_second,
        down_updated,
        gains_first,
        gains_second,
        gains_updated,
    )


def solution(mesh):
    in_specs = (
        P(("dp", "tensor"), None),
        P(("dp", "tensor"), None),
        P("dp", None),
        P(None, None, "tensor"),
        P(None, None, "tensor"),
        P(None, None, "tensor"),
        P("tensor", None),
        P("tensor", None),
        P("tensor", None),
        P(None, None, "tensor"),
        P(None, None, "tensor"),
        P(None, None, "tensor"),
        P("tensor", None),
        P("tensor", None),
        P("tensor", None),
        P(),
        P(),
        P(),
    )
    out_specs = (
        P(("dp", "tensor"), None),
        P(("dp", "tensor"), None),
        P(None, None, "tensor"),
        P(None, None, "tensor"),
        P(None, None, "tensor"),
        P("tensor", None),
        P("tensor", None),
        P("tensor", None),
        P(None, None, "tensor"),
        P(None, None, "tensor"),
        P(None, None, "tensor"),
        P("tensor", None),
        P("tensor", None),
        P("tensor", None),
        P(),
        P(),
        P(),
    )
    return jax.shard_map(shards, mesh=mesh, in_specs=in_specs, out_specs=out_specs, check_vma=False)
```
